32 devices in a mesh: row: 4 (over z), col: 8 (over y, x, core).
Axes of the slice: x: 2, y: 2, z: 4, core: 2. Of those that a mesh axis runs over, the one named last changes fastest.
Arguments:
- object_field: float32 [2, 4, 1024, 2048], P(None, None, 'row', 'col'), may hold values from -4 to 4
- probe: float32 [2, 4, 128, 128], replicated, may hold values from -6 to 6
- amplitudes: float32 [4, 8, 5, 128, 128], P('row', 'col'), may hold values from 0.2 to 4
- offsets: int32 [4, 8, 5, 2], P('row', 'col'), may hold values from 0 to 1920, as said below
- counts: int32 [4, 8], P('row', 'col'), may hold values from 1 to 5, as said below
Outputs:
- new_object: float32 [2, 4, 1024, 2048], P(None, None, 'row', 'col')
- new_probe: float32 [2, 4, 128, 128], replicated
The draws below stay inside these ranges and needn't reach their ends.
Inputs may be any that keep to these rules, and one draw needn't show every extreme that they name: `offsets`: slot k of device (a, b) has corner (y, x) with a * 256 <= y < (a + 1) * 256, b * 256 <= x < (b + 1) * 256, y <= 896 and x <= 1920; dead slots hold such corners too. Slots k >= counts of a device are dead; some device has all 5 slots live.
All inputs are finite; a program needn't handle non-finite values.
Results may differ from the reference program's by a relative error of at most 0.00019.
Values sent between devices are 32-bit elements; how exact they have to be, the bound alone decides.
A program may use at most 128 MiB of HBM per device.

```python
import math
import jax
import jax.numpy as jnp
from jax import lax

P_SIZE = 128
MODES = 4
SLICES = 4
TR = 256
TC = 256
CAP = 5
NR = 1024
NC = 2048
N_ROW = 4
N_COL = 8


def draw_offsets(key, part):
    key = jax.random.fold_in(key, 11)
    key_rows, key_cols = jax.random.split(key)
    band_rows = NR // TR
    band_cols = NC // TC
    row_band = jnp.arange(band_rows, dtype=jnp.int32)[:, None, None]
    col_band = jnp.arange(band_cols, dtype=jnp.int32)[None, :, None]
    row_room = jnp.minimum(TR, NR - P_SIZE - row_band * TR + 1)
    col_room = jnp.minimum(TC, NC - P_SIZE - col_band * TC + 1)
    row_pick = jax.random.randint(key_rows, (band_rows, band_cols, CAP), 0, row_room)
    col_pick = jax.random.randint(key_cols, (band_rows, band_cols, CAP), 0, col_room)
    corners = jnp.stack([row_band * TR + row_pick, col_band * TC + col_pick], axis=-1).astype(jnp.int32)
    corners = corners.at[0, 0, 0].set(jnp.array([0, 0], jnp.int32))
    corners = corners.at[band_rows - 1, band_cols - 1, 0].set(jnp.array([NR - P_SIZE, NC - P_SIZE], jnp.int32))
    return corners.astype(jnp.int32)


def draw_counts(key, part):
    key = jax.random.fold_in(key, 12)
    key_base, key_full = jax.random.split(key)
    band_rows = NR // TR
    band_cols = NC // TC
    base_counts = jax.random.randint(key_base, (band_rows * band_cols,), 1, CAP + 1)
    full_device = jax.random.randint(key_full, (), 0, band_rows * band_cols)
    device_ids = jnp.arange(band_rows * band_cols, dtype=jnp.int32)
    filled = jnp.where(device_ids == full_device, CAP, base_counts)
    return filled.reshape(band_rows, band_cols).astype(jnp.int32)


def shard_levels(rng, extent, cuts, low, largest):
    factor_of, own = 1.0, jax.random.fold_in(rng, 6)
    for dim, parts in cuts:
        heights = jnp.exp(jax.random.uniform(jax.random.fold_in(own, dim), (parts,), jnp.float32, low / len(cuts), largest / len(cuts)))
        factor_of = factor_of * jnp.repeat(heights, extent[dim] // parts).reshape([-1 if axis == dim else 1 for axis in range(len(extent))])
    return factor_of


def gaussian(key, shape, deviation, reach, pieces=(), held_as=jnp.bfloat16):
    values = jax.random.normal(key, shape, jnp.float32) * deviation
    if len(pieces) > 0:
        values = shard_levels(key, shape, pieces, -0.22, 0.18) * values
    return jnp.clip(values, min=-reach, max=reach).astype(held_as)


def setup_inputs(seed: int = 0) -> dict:
    streams_of = jax.random.split(jax.random.key(seed), 6)
    return {
        "object_field": gaussian(streams_of[0], (2, SLICES, NR, NC), 0.6, 4.0, ((2, 4), (3, 8)), jnp.float32),
        "probe": gaussian(streams_of[1], (2, MODES, P_SIZE, P_SIZE), 1.0, 6.0, (), jnp.float32),
        "amplitudes": jnp.clip(jnp.exp(math.log(4.0) - 2.9957323 * jax.random.uniform(streams_of[2], (N_ROW, N_COL, CAP, P_SIZE, P_SIZE), jnp.float32) ** shard_levels(streams_of[2], (N_ROW, N_COL, CAP, P_SIZE, P_SIZE), ((0, 4), (1, 8)), -0.2, 0.2)), 0.2, 4.0),
        "offsets": draw_offsets(jax.random.fold_in(streams_of[5], 71), 0),
        "counts": draw_counts(jax.random.fold_in(streams_of[5], 71), 0),
    }


FRESNEL = 4.0
STEP_OBJECT = 0.5
STEP_PROBE = 0.5

def transfer_kernel(points):
    frequency = jnp.fft.fftfreq(points).astype(jnp.float32)
    phase = -jnp.pi * FRESNEL * (frequency[:, None] ** 2 + frequency[None, :] ** 2)
    return lax.complex(jnp.cos(phase), jnp.sin(phase))

def position_loss(window, probe, amplitude, kernel):
    object_slices = lax.complex(window[0], window[1])
    wavefield = lax.complex(probe[0], probe[1])
    for slice_index in range(SLICES):
        wavefield = wavefield * object_slices[slice_index]
        if slice_index < SLICES - 1:
            spectrum = jnp.fft.fft2(wavefield, norm='ortho') * kernel
            wavefield = jnp.fft.ifft2(spectrum, norm='ortho')
    far_field = jnp.fft.fft2(wavefield, norm='ortho')
    intensity = lax.optimization_barrier(jnp.sum(jnp.real(far_field) ** 2 + jnp.imag(far_field) ** 2, axis=0))
    return jnp.sum((jnp.sqrt(intensity + 1.0) - amplitude) ** 2)

def reference(object_field, probe, amplitudes, offsets, counts):
    kernel = transfer_kernel(P_SIZE)
    flat_offsets = offsets.reshape(-1, 2).astype(jnp.int32)
    flat_amplitudes = amplitudes.reshape(-1, P_SIZE, P_SIZE)
    live_slots = (jnp.arange(CAP, dtype=jnp.int32)[None, None, :] < counts[:, :, None]).reshape(-1).astype(jnp.float32)
    zero_index = jnp.zeros((), jnp.int32)

    def accumulate(carry, item):
        grad_object, grad_probe, weight = carry
        position, amplitude, alive = item
        starts = (zero_index, zero_index, position[0], position[1])
        window = lax.dynamic_slice(object_field, starts, (2, SLICES, P_SIZE, P_SIZE))

        def local_loss(window_part, probe_part):
            return position_loss(window_part, probe_part, amplitude, kernel)
        loss_value, pull_back = jax.vjp(local_loss, window, probe)
        grad_window, grad_wave = pull_back(alive)
        previous = lax.dynamic_slice(grad_object, starts, (2, SLICES, P_SIZE, P_SIZE))
        grad_object = lax.dynamic_update_slice(grad_object, previous + grad_window, starts)
        weight = weight + alive * (window[0, 0] ** 2 + window[1, 0] ** 2)
        return ((grad_object, grad_probe + grad_wave, weight), None)
    initial = (jnp.zeros_like(object_field), jnp.zeros_like(probe), jnp.zeros((P_SIZE, P_SIZE), jnp.float32))
    totals, unused = lax.scan(accumulate, initial, (flat_offsets, flat_amplitudes, live_slots))
    grad_object, grad_probe, weight = totals
    new_object = object_field - STEP_OBJECT * grad_object
    new_probe = probe - STEP_PROBE * grad_probe / (weight + 1.0)
    return (new_object, new_probe)
```

```python
from functools import partial
import math

import jax
import jax.numpy as jnp
import ml_dtypes
import numpy as np
from jax import lax
from jax.experimental import pallas as pl
from jax.experimental.pallas import tpu as pltpu
from jax.sharding import PartitionSpec as P

FRESNEL = 4.0
STEP_OBJECT = 0.5
STEP_PROBE = 0.5
ROWS = 8


def tables(points):
    position = np.arange(points)
    angle = -2.0 * np.pi / points * (position[:, None] * position[None, :] % points)
    dft = np.exp(1j * angle) / math.sqrt(points)
    frequency = np.where(position < points // 2, position, position - points) / points
    propagator = np.conj(dft) @ (np.exp(-1j * np.pi * FRESNEL * frequency**2)[:, None] * dft)

    def split(matrix):
        high = matrix.astype(np.float32).astype(ml_dtypes.bfloat16)
        low = (matrix - high.astype(np.float64)).astype(np.float32).astype(ml_dtypes.bfloat16)
        return high, low

    lefts, rights = [], []
    for matrix in (propagator, np.conj(propagator), dft, np.conj(dft)):
        real, imag = matrix.real, matrix.imag
        high, low = split(np.block([[real, -imag], [imag, real]]))
        lefts.append(np.concatenate([high, high, low], axis=1))
        high, low = split(np.block([[real, imag], [-imag, real]]))
        rights.append(np.concatenate([high, high, low], axis=0))
    return np.stack(lefts), np.stack(rights)


def split(value):
    high = value.astype(jnp.bfloat16)
    return high, (value - high.astype(jnp.float32)).astype(jnp.bfloat16)


def grid(blocks):
    return jnp.concatenate([jnp.concatenate(row, axis=1) for row in blocks], axis=0)


def left_product(weight, pair):
    n = pair[0].shape[0]
    (r0, r0l), (r1, r1l), (i0, i0l), (i1, i1l) = map(split, pair)
    x = grid([[r0, r1], [i0, i1], [r0l, r1l], [i0l, i1l], [r0, r1], [i0, i1]])
    y = jnp.dot(weight, x, preferred_element_type=jnp.float32)
    return y[:n, :n], y[:n, n:], y[n:, :n], y[n:, n:]


def right_product(weight, pair):
    n = pair[0].shape[0]
    (r0, r0l), (r1, r1l), (i0, i0l), (i1, i1l) = map(split, pair)
    x = grid([[r0, i0, r0l, i0l, r0, i0], [r1, i1, r1l, i1l, r1, i1]])
    y = jnp.dot(x, weight, preferred_element_type=jnp.float32)
    return y[:n, :n], y[n:, :n], y[:n, n:], y[n:, n:]


def times(pair, obj):
    (r0, r1, i0, i1), (a, b) = pair, obj
    return r0 * a - i0 * b, r1 * a - i1 * b, r0 * b + i0 * a, r1 * b + i1 * a


def times_conj(pair, obj):
    return times(pair, (obj[0], -obj[1]))


def positions(
    counts_ref, offsets_ref, obj_hbm, below_hbm, right_hbm, corner_hbm, probe_ref, amp_ref, lefts, rights,
    new_hbm, low_hbm, side_hbm, edge_hbm, sums_ref, ext, acc, window, waves, sems,
):
    depth, rows, cols = obj_hbm.shape[1:]
    n = probe_ref.shape[2]
    modes = probe_ref.shape[1]
    pairs = modes // 2
    slots = amp_ref.shape[0]
    parts = (
        (slice(0, rows), slice(0, cols)),
        (slice(rows, rows + n), slice(0, cols)),
        (slice(0, rows), slice(cols, cols + n)),
        (slice(rows, rows + n), slice(cols, cols + n)),
    )
    loads = [
        pltpu.make_async_copy(source, ext.at[:, :, r, c], sems.at[i])
        for i, (source, (r, c)) in enumerate(zip((obj_hbm, below_hbm, right_hbm, corner_hbm), parts))
    ]
    for copy in loads:
        copy.start()
    acc[...] = jnp.zeros_like(acc)
    sums_ref[...] = jnp.zeros_like(sums_ref)
    for copy in loads:
        copy.wait()
    tall = n + ROWS
    lane = lax.broadcasted_iota(jnp.int32, (tall, n), 1)

    def keep(level, p, pair):
        for c in range(2):
            for j in range(2):
                waves[level, c, 2 * p + j] = pair[2 * c + j]

    def kept(level, p):
        source = probe_ref if level == 0 else waves.at[level - 1]
        return tuple(source[c, 2 * p + j] for c in range(2) for j in range(2))

    @pl.loop(0, slots)
    def _(k):
        @pl.when(k < counts_ref[0, 0])
        def _():
            y = offsets_ref[0, 0, k, 0] % rows
            x = offsets_ref[0, 0, k, 1] % cols
            base = pl.multiple_of(x // n * n, n)
            step = x % n
            top = pl.multiple_of(y // ROWS * ROWS, ROWS)
            drop = y % ROWS
            for s in range(depth):
                for c in range(2):
                    near = ext[c, s, pl.ds(top, tall), pl.ds(base, n)]
                    far = ext[c, s, pl.ds(top, tall), pl.ds(base + n, n)]
                    turned = pltpu.roll(jnp.where(lane >= step, near, far), (n - step) % n, 1)
                    window[c, s] = pltpu.roll(turned, (tall - drop) % tall, 0)[:n]
            sums_ref[2 * modes] += window[0, 0] ** 2 + window[1, 0] ** 2

            state = [kept(0, p) for p in range(pairs)]
            for s in range(depth):
                obj = (window[0, s], window[1, s])
                state = [times(pair, obj) for pair in state]
                which = 0 if s < depth - 1 else 2
                state = [left_product(lefts[which], pair) for pair in state]
                state = [right_product(rights[which], pair) for pair in state]
                if s < depth - 1:
                    for p in range(pairs):
                        keep(s, p, state[p])
            intensity = sum(v * v for pair in state for v in pair)
            factor = 2.0 - 2.0 * amp_ref[k] / jnp.sqrt(intensity + 1.0)
            state = [tuple(v * factor for v in pair) for pair in state]
            for s in range(depth - 1, -1, -1):
                which = 1 if s < depth - 1 else 3
                state = [left_product(lefts[which], pair) for pair in state]
                state = [right_product(rights[which], pair) for pair in state]
                grads = [0.0, 0.0]
                for p in range(pairs):
                    w = kept(s, p)
                    g = state[p]
                    for j in range(2):
                        grads[0] += g[j] * w[j] + g[2 + j] * w[2 + j]
                        grads[1] += g[2 + j] * w[j] - g[j] * w[2 + j]
                for c in range(2):
                    moved = jnp.concatenate([grads[c] * STEP_OBJECT, jnp.zeros((ROWS, n), jnp.float32)], axis=0)
                    moved = pltpu.roll(pltpu.roll(moved, drop, 0), step, 1)
                    acc[c, s, pl.ds(top, tall), pl.ds(base, n)] += jnp.where(lane >= step, moved, 0.0)
                    acc[c, s, pl.ds(top, tall), pl.ds(base + n, n)] += jnp.where(lane >= step, 0.0, moved)
                obj = (window[0, s], window[1, s])
                state = [times_conj(pair, obj) for pair in state]
            for p in range(pairs):
                for c in range(2):
                    for j in range(2):
                        sums_ref[c * modes + 2 * p + j] += state[p][2 * c + j]

    r, c = parts[0]
    acc[:, :, r, c] = ext[:, :, r, c] - acc[:, :, r, c]
    stores = [
        pltpu.make_async_copy(acc.at[:, :, r, c], target, sems.at[i])
        for i, (target, (r, c)) in enumerate(zip((new_hbm, low_hbm, side_hbm, edge_hbm), parts))
    ]
    for copy in stores:
        copy.start()
    for copy in stores:
        copy.wait()


def shards(n_row, n_col, object_field, probe, amplitudes, offsets, counts):
    _, depth, rows, cols = object_field.shape
    modes, n = probe.shape[1:3]

    def shift(value, down, across, sign):
        pairs = []
        for a in range(n_row - down):
            for b in range(n_col - across):
                pair = ((a + down) * n_col + b + across, a * n_col + b)
                pairs.append(pair[::sign])
        return lax.ppermute(value, ("row", "col"), pairs)

    below = shift(object_field[:, :, :n, :], 1, 0, 1)
    right = shift(object_field[:, :, :, :n], 0, 1, 1)
    corner = shift(object_field[:, :, :n, :n], 1, 1, 1)
    lefts, rights = tables(n)
    f32 = jnp.float32
    vmem = pl.BlockSpec(memory_space=pltpu.VMEM)
    smem = pl.BlockSpec(memory_space=pltpu.SMEM)
    hbm = pl.BlockSpec(memory_space=pl.ANY)
    flops = amplitudes.shape[2] * depth * 4 * 2 * (modes * n) * (6 * n) * (2 * n)
    part, low, side, edge, sums = pl.pallas_call(
        positions,
        out_shape=(
            jax.ShapeDtypeStruct((2, depth, rows, cols), f32),
            jax.ShapeDtypeStruct((2, depth, n, cols), f32),
            jax.ShapeDtypeStruct((2, depth, rows, n), f32),
            jax.ShapeDtypeStruct((2, depth, n, n), f32),
            jax.ShapeDtypeStruct((2 * modes + 1, n, n), f32),
        ),
        in_specs=[smem, smem, hbm, hbm, hbm, hbm, vmem, vmem, vmem, vmem],
        out_specs=(hbm, hbm, hbm, hbm, vmem),
        scratch_shapes=[
            pltpu.VMEM((2, depth, rows + n, cols + n), f32),
            pltpu.VMEM((2, depth, rows + n, cols + n), f32),
            pltpu.VMEM((2, depth, n, n), f32),
            pltpu.VMEM((depth - 1, 2, modes, n, n), f32),
            pltpu.SemaphoreType.DMA((4,)),
        ],
        compiler_params=pltpu.CompilerParams(vmem_limit_bytes=48 * 2**20),
        cost_estimate=pl.CostEstimate(flops=flops, bytes_accessed=20 * 2**20, transcendentals=0),
        name="positions",
    )(counts, offsets, object_field, below, right, corner, probe, amplitudes[0, 0], jnp.asarray(lefts), jnp.asarray(rights))
    totals = lax.psum(sums, ("row", "col"))
    low = shift(low, 1, 0, -1)
    side = shift(side, 0, 1, -1)
    edge = shift(edge, 1, 1, -1)

    def widen(value):
        gaps = [(0, 0, 0), (0, 0, 0), (0, rows - value.shape[2], 0), (0, cols - value.shape[3], 0)]
        return lax.pad(value, jnp.zeros((), f32), gaps)

    new_object = part - widen(low) - widen(side) - widen(edge)
    grad_total = totals[: 2 * modes].reshape(probe.shape)
    new_probe = probe - STEP_PROBE * grad_total / (totals[2 * modes] + 1.0)
    return (new_object, new_probe)


def solution(mesh):
    return jax.shard_map(
        partial(shards, mesh.shape["row"], mesh.shape["col"]),
        mesh=mesh,
        in_specs=(
            P(None, None, "row", "col"),
            P(),
            P("row", "col", None, None, None),
            P("row", "col", None, None),
            P("row", "col"),
        ),
        out_specs=(P(None, None, "row", "col"), P()),
        check_vma=False,
    )
```

```python
from functools import partial
import math

import jax
import jax.numpy as jnp
import ml_dtypes
import numpy as np
from jax import lax
from jax.experimental import pallas as pl
from jax.experimental.pallas import tpu as pltpu
from jax.sharding import PartitionSpec as P

FRESNEL = 4.0
STEP_OBJECT = 0.5
STEP_PROBE = 0.5
ROWS = 8


def tables(points):
    position = np.arange(points)
    angle = -2.0 * np.pi / points * (position[:, None] * position[None, :] % points)
    dft = np.exp(1j * angle) / math.sqrt(points)
    frequency = np.where(position < points // 2, position, position - points) / points
    propagator = np.conj(dft) @ (np.exp(-1j * np.pi * FRESNEL * frequency**2)[:, None] * dft)

    def split(matrix):
        high = matrix.astype(np.float32).astype(ml_dtypes.bfloat16)
        low = (matrix - high.astype(np.float64)).astype(np.float32).astype(ml_dtypes.bfloat16)
        return high, low

    lefts, rights = [], []
    for matrix in (propagator, np.conj(propagator), dft, np.conj(dft)):
        real, imag = matrix.real, matrix.imag
        high, low = split(np.block([[real, -imag], [imag, real]]))
        lefts.append(np.concatenate([high, high, low], axis=1))
        high, low = split(np.block([[real, imag], [-imag, real]]))
        rights.append(np.concatenate([high, high, low], axis=0))
    return np.stack(lefts), np.stack(rights)


def split(value):
    high = value.astype(jnp.bfloat16)
    return high, (value - high.astype(jnp.float32)).astype(jnp.bfloat16)


def grid(blocks):
    return jnp.concatenate([jnp.concatenate(row, axis=1) for row in blocks], axis=0)


def left_product(weight, pair):
    n = pair[0].shape[0]
    (r0, r0l), (r1, r1l), (i0, i0l), (i1, i1l) = map(split, pair)
    x = grid([[r0, r1], [i0, i1], [r0l, r1l], [i0l, i1l], [r0, r1], [i0, i1]])
    y = jnp.dot(weight, x, preferred_element_type=jnp.float32)
    return y[:n, :n], y[:n, n:], y[n:, :n], y[n:, n:]


def right_product(weight, pair):
    n = pair[0].shape[0]
    (r0, r0l), (r1, r1l), (i0, i0l), (i1, i1l) = map(split, pair)
    x = grid([[r0, i0, r0l, i0l, r0, i0], [r1, i1, r1l, i1l, r1, i1]])
    y = jnp.dot(x, weight, preferred_element_type=jnp.float32)
    return y[:n, :n], y[n:, :n], y[:n, n:], y[n:, n:]


def times(pair, obj):
    (r0, r1, i0, i1), (a, b) = pair, obj
    return r0 * a - i0 * b, r1 * a - i1 * b, r0 * b + i0 * a, r1 * b + i1 * a


def times_conj(pair, obj):
    return times(pair, (obj[0], -obj[1]))


def positions(
    counts_ref, offsets_ref, obj_hbm, below_hbm, right_hbm, corner_hbm, probe_ref, amp_ref, lefts, rights,
    new_hbm, low_hbm, side_hbm, edge_hbm, sums_ref, ext, acc, window, waves, sems,
):
    depth, rows, cols = obj_hbm.shape[1:]
    n = probe_ref.shape[2]
    modes = probe_ref.shape[1]
    pairs = modes // 2
    slots = amp_ref.shape[0]
    parts = (
        (slice(0, rows), slice(0, cols)),
        (slice(rows, rows + n), slice(0, cols)),
        (slice(0, rows), slice(cols, cols + n)),
        (slice(rows, rows + n), slice(cols, cols + n)),
    )
    loads = [
        pltpu.make_async_copy(source, ext.at[:, :, r, c], sems.at[i])
        for i, (source, (r, c)) in enumerate(zip((obj_hbm, below_hbm, right_hbm, corner_hbm), parts))
    ]
    for copy in loads:
        copy.start()
    acc[...] = jnp.zeros_like(acc)
    sums_ref[...] = jnp.zeros_like(sums_ref)
    for copy in loads:
        copy.wait()
    tall = n + ROWS
    lane = lax.broadcasted_iota(jnp.int32, (tall, n), 1)

    def keep(level, p, pair):
        for c in range(2):
            for j in range(2):
                waves[level, c, 2 * p + j] = pair[2 * c + j]

    def kept(level, p):
        source = probe_ref if level == 0 else waves.at[level - 1]
        return tuple(source[c, 2 * p + j] for c in range(2) for j in range(2))

    @pl.loop(0, slots)
    def _(k):
        @pl.when(k < counts_ref[0, 0])
        def _():
            y = offsets_ref[0, 0, k, 0] % rows
            x = offsets_ref[0, 0, k, 1] % cols
            base = pl.multiple_of(x // n * n, n)
            step = x % n
            top = pl.multiple_of(y // ROWS * ROWS, ROWS)
            drop = y % ROWS
            for s in range(depth):
                for c in range(2):
                    near = ext[c, s, pl.ds(top, tall), pl.ds(base, n)]
                    far = ext[c, s, pl.ds(top, tall), pl.ds(base + n, n)]
                    turned = pltpu.roll(jnp.where(lane >= step, near, far), (n - step) % n, 1)
                    window[c, s] = pltpu.roll(turned, (tall - drop) % tall, 0)[:n]
            sums_ref[pl.ds(2 * modes * n, n)] += window[0, 0] ** 2 + window[1, 0] ** 2

            state = [kept(0, p) for p in range(pairs)]
            for s in range(depth):
                obj = (window[0, s], window[1, s])
                state = [times(pair, obj) for pair in state]
                which = 0 if s < depth - 1 else 2
                state = [left_product(lefts[which], pair) for pair in state]
                state = [right_product(rights[which], pair) for pair in state]
                if s < depth - 1:
                    for p in range(pairs):
                        keep(s, p, state[p])
            intensity = sum(v * v for pair in state for v in pair)
            factor = 2.0 - 2.0 * amp_ref[k] / jnp.sqrt(intensity + 1.0)
            state = [tuple(v * factor for v in pair) for pair in state]
            for s in range(depth - 1, -1, -1):
                which = 1 if s < depth - 1 else 3
                state = [left_product(lefts[which], pair) for pair in state]
                state = [right_product(rights[which], pair) for pair in state]
                grads = [0.0, 0.0]
                for p in range(pairs):
                    w = kept(s, p)
                    g = state[p]
                    for j in range(2):
                        grads[0] += g[j] * w[j] + g[2 + j] * w[2 + j]
                        grads[1] += g[2 + j] * w[j] - g[j] * w[2 + j]
                for c in range(2):
                    moved = jnp.concatenate([grads[c] * STEP_OBJECT, jnp.zeros((ROWS, n), jnp.float32)], axis=0)
                    moved = pltpu.roll(pltpu.roll(moved, drop, 0), step, 1)
                    acc[c, s, pl.ds(top, tall), pl.ds(base, n)] += jnp.where(lane >= step, moved, 0.0)
                    acc[c, s, pl.ds(top, tall), pl.ds(base + n, n)] += jnp.where(lane >= step, 0.0, moved)
                obj = (window[0, s], window[1, s])
                state = [times_conj(pair, obj) for pair in state]
            for p in range(pairs):
                for c in range(2):
                    for j in range(2):
                        sums_ref[pl.ds((c * modes + 2 * p + j) * n, n)] += state[p][2 * c + j]

    r, c = parts[0]
    acc[:, :, r, c] = ext[:, :, r, c] - acc[:, :, r, c]
    stores = [
        pltpu.make_async_copy(acc.at[:, :, r, c], target, sems.at[i])
        for i, (target, (r, c)) in enumerate(zip((new_hbm, low_hbm, side_hbm, edge_hbm), parts))
    ]
    for copy in stores:
        copy.start()
    for copy in stores:
        copy.wait()


def remote(source, target, send, recv, device):
    return pltpu.make_async_remote_copy(
        src_ref=source, dst_ref=target, send_sem=send, recv_sem=recv,
        device_id=device, device_id_type=pl.DeviceIdType.MESH,
    )


def signal(device):
    pl.semaphore_signal(
        pltpu.get_barrier_semaphore(), inc=1, device_id=device, device_id_type=pl.DeviceIdType.MESH
    )


def gather(n_row, n_col, obj, below, right, corner, send, recv):
    a, b = lax.axis_index("row"), lax.axis_index("col")
    depth, n = below.shape[1:3]
    has_up, has_down, has_left, has_right = a > 0, a < n_row - 1, b > 0, b < n_col - 1
    up, left = (a - 1, b), (a, b - 1)
    barrier = pltpu.get_barrier_semaphore()

    @pl.when(has_down)
    def _():
        signal((a + 1, b))

    @pl.when(has_right)
    def _():
        signal((a, b + 1))

    rows = [
        remote(obj.at[:, s, pl.ds(0, n), :], below.at[:, s], send.at[0, s], recv.at[0, s], up) for s in range(depth)
    ]
    side = remote(obj.at[:, :, :, pl.ds(0, n)], right, send.at[1, 0], recv.at[1, 0], left)
    edges = [
        remote(below.at[:, s, :, pl.ds(0, n)], corner.at[:, s], send.at[2, s], recv.at[2, s], left)
        for s in range(depth)
    ]

    @pl.when(has_up & has_left)
    def _():
        pl.semaphore_wait(barrier, 2)

    @pl.when(has_up != has_left)
    def _():
        pl.semaphore_wait(barrier, 1)

    @pl.when(has_up)
    def _():
        for copy in rows:
            copy.start()

    @pl.when(has_left)
    def _():
        side.start()

    for s in range(depth):

        @pl.when(has_down)
        def _():
            rows[s].wait_recv()

        @pl.when(has_down & has_left)
        def _():
            edges[s].start()

    @pl.when(has_right)
    def _():
        side.wait_recv()

    @pl.when(has_down & has_right)
    def _():
        for copy in edges:
            copy.wait_recv()

    @pl.when(has_up)
    def _():
        for copy in rows:
            copy.wait_send()

    @pl.when(has_left)
    def _():
        side.wait_send()

    @pl.when(has_down & has_left)
    def _():
        for copy in edges:
            copy.wait_send()


def finish(
    n_row, n_col, part, low, side, edge, sums, probe, new_object, new_probe,
    low_out, low_in, side_in, edge_in, first, middle, second, total,
    send, recv, col_send, col_recv, row_send, row_recv,
):
    a, b = lax.axis_index("row"), lax.axis_index("col")
    depth, n = low.shape[1:3]
    modes = probe.shape[1]
    big = middle.shape[0]
    small = big // n_row
    has_up, has_down, has_left, has_right = a > 0, a < n_row - 1, b > 0, b < n_col - 1
    col_peers = [lax.rem(b + i, n_col) for i in range(1, n_col)]
    row_peers = [lax.rem(a + i, n_row) for i in range(1, n_row)]
    barrier = pltpu.get_barrier_semaphore()
    for peer in col_peers:
        signal((a, peer))
    for peer in row_peers:
        signal((peer, b))
    pl.semaphore_wait(barrier, n_col - 1 + n_row - 1)

    def chunk(ref, index, size):
        return ref.at[pl.ds(pl.multiple_of(index * size, ROWS), size)]

    scatter_col = [
        remote(chunk(sums, peer, big), first.at[i], col_send.at[0, i], col_recv.at[0, i], (a, peer))
        for i, peer in enumerate(col_peers)
    ]
    for copy in scatter_col:
        copy.start()
    right, down = (a, b + 1), (a + 1, b)
    edges = [remote(edge.at[:, s], edge_in.at[:, s], send.at[0, s], recv.at[0, s], right) for s in range(depth)]
    sides = remote(side, side_in, send.at[1, 0], recv.at[1, 0], right)
    lows = [remote(low_out.at[:, s], low_in.at[:, s], send.at[2, s], recv.at[2, s], down) for s in range(depth)]

    @pl.when(has_down & has_right)
    def _():
        for copy in edges:
            copy.start()

    @pl.when(has_right)
    def _():
        sides.start()

    for s in range(depth):
        low_out[:, s] = low[:, s]

        @pl.when(has_down & has_left)
        def _():
            edges[s].wait_recv()
            low_out[:, s, :, :n] += edge_in[:, s]

        @pl.when(has_down)
        def _():
            lows[s].start()

    for copy in scatter_col:
        copy.wait()
    mine = chunk(sums, b, big)[...]
    for i in range(n_col - 1):
        mine += first[i]
    middle[...] = mine
    scatter_row = [
        remote(chunk(middle, peer, small), second.at[i], row_send.at[0, i], row_recv.at[0, i], (peer, b))
        for i, peer in enumerate(row_peers)
    ]
    for copy in scatter_row:
        copy.start()
    for copy in scatter_row:
        copy.wait()
    mine = chunk(middle, a, small)[...]
    for i in range(n_row - 1):
        mine += second[i]
    own = chunk(total, b * n_row + a, small)
    own[...] = mine
    gather_row = [
        remote(own, own, row_send.at[1, i], row_recv.at[1, i], (peer, b)) for i, peer in enumerate(row_peers)
    ]
    for copy in gather_row:
        copy.start()
    for copy in gather_row:
        copy.wait()
    group = chunk(total, b, big)
    gather_col = [
        remote(group, group, col_send.at[1, i], col_recv.at[1, i], (a, peer)) for i, peer in enumerate(col_peers)
    ]
    for copy in gather_col:
        copy.start()
    new_object[...] = part[...]

    @pl.when(has_left)
    def _():
        sides.wait_recv()
        new_object[:, :, :, :n] -= side_in[...]

    for s in range(depth):

        @pl.when(has_up)
        def _():
            lows[s].wait_recv()
            new_object[:, s, :n] -= low_in[:, s]

    for copy in gather_col:
        copy.wait()
    scale = STEP_PROBE / (total[pl.ds(2 * modes * n, n)] + 1.0)
    for c in range(2):
        for m in range(modes):
            new_probe[c, m] = probe[c, m] - total[pl.ds((c * modes + m) * n, n)] * scale

    @pl.when(has_down & has_right)
    def _():
        for copy in edges:
            copy.wait_send()

    @pl.when(has_right)
    def _():
        sides.wait_send()

    @pl.when(has_down)
    def _():
        for copy in lows:
            copy.wait_send()


def shards(n_row, n_col, object_field, probe, amplitudes, offsets, counts):
    _, depth, rows, cols = object_field.shape
    modes, n = probe.shape[1:3]
    f32 = jnp.float32
    vmem = pl.BlockSpec(memory_space=pltpu.VMEM)
    smem = pl.BlockSpec(memory_space=pltpu.SMEM)
    hbm = pl.BlockSpec(memory_space=pl.ANY)
    rims = (
        jax.ShapeDtypeStruct((2, depth, n, cols), f32),
        jax.ShapeDtypeStruct((2, depth, rows, n), f32),
        jax.ShapeDtypeStruct((2, depth, n, n), f32),
    )
    dma = pltpu.SemaphoreType.DMA
    below, right, corner = pl.pallas_call(
        partial(gather, n_row, n_col),
        out_shape=rims,
        in_specs=[hbm],
        out_specs=(hbm, hbm, hbm),
        scratch_shapes=[dma((3, depth)), dma((3, depth))],
        compiler_params=pltpu.CompilerParams(collective_id=0, has_side_effects=True),
        name="gather",
    )(object_field)
    lefts, rights = tables(n)
    flops = amplitudes.shape[2] * depth * 4 * 2 * (modes * n) * (6 * n) * (2 * n)
    devices = n_row * n_col
    small = -(-(2 * modes + 1) * n // (devices * ROWS)) * ROWS
    part, low, side, edge, sums = pl.pallas_call(
        positions,
        out_shape=(
            jax.ShapeDtypeStruct((2, depth, rows, cols), f32),
            *rims,
            jax.ShapeDtypeStruct((devices * small, n), f32),
        ),
        in_specs=[smem, smem, hbm, hbm, hbm, hbm, vmem, vmem, vmem, vmem],
        out_specs=(hbm, hbm, hbm, hbm, vmem),
        scratch_shapes=[
            pltpu.VMEM((2, depth, rows + n, cols + n), f32),
            pltpu.VMEM((2, depth, rows + n, cols + n), f32),
            pltpu.VMEM((2, depth, n, n), f32),
            pltpu.VMEM((depth - 1, 2, modes, n, n), f32),
            dma((4,)),
        ],
        compiler_params=pltpu.CompilerParams(vmem_limit_bytes=56 * 2**20),
        cost_estimate=pl.CostEstimate(flops=flops, bytes_accessed=20 * 2**20, transcendentals=0),
        name="positions",
    )(counts, offsets, object_field, below, right, corner, probe, amplitudes[0, 0], jnp.asarray(lefts), jnp.asarray(rights))
    return pl.pallas_call(
        partial(finish, n_row, n_col),
        out_shape=(
            jax.ShapeDtypeStruct(object_field.shape, f32),
            jax.ShapeDtypeStruct(probe.shape, f32),
        ),
        in_specs=[vmem] * 6,
        out_specs=(vmem, vmem),
        scratch_shapes=[
            pltpu.VMEM(rims[0].shape, f32),
            pltpu.VMEM(rims[0].shape, f32),
            pltpu.VMEM(rims[1].shape, f32),
            pltpu.VMEM(rims[2].shape, f32),
            pltpu.VMEM((n_col - 1, n_row * small, n), f32),
            pltpu.VMEM((n_row * small, n), f32),
            pltpu.VMEM((n_row - 1, small, n), f32),
            pltpu.VMEM((devices * small, n), f32),
            dma((3, depth)),
            dma((3, depth)),
            dma((2, n_col - 1)),
            dma((2, n_col - 1)),
            dma((2, n_row - 1)),
            dma((2, n_row - 1)),
        ],
        compiler_params=pltpu.CompilerParams(
            collective_id=1, has_side_effects=True, vmem_limit_bytes=40 * 2**20
        ),
        name="finish",
    )(part, low, side, edge, sums, probe)


def solution(mesh):
    return jax.shard_map(
        partial(shards, mesh.shape["row"], mesh.shape["col"]),
        mesh=mesh,
        in_specs=(
            P(None, None, "row", "col"),
            P(),
            P("row", "col", None, None, None),
            P("row", "col", None, None),
            P("row", "col"),
        ),
        out_specs=(P(None, None, "row", "col"), P()),
        check_vma=False,
    )
```

```python
from functools import partial
import math

import jax
import jax.numpy as jnp
import ml_dtypes
import numpy as np
from jax import lax
from jax.experimental import pallas as pl
from jax.experimental.pallas import tpu as pltpu
from jax.sharding import PartitionSpec as P

FRESNEL = 4.0
STEP_OBJECT = 0.5
STEP_PROBE = 0.5
ROWS = 8


def tables(points):
    position = np.arange(points)
    angle = -2.0 * np.pi / points * (position[:, None] * position[None, :] % points)
    dft = np.exp(1j * angle) / math.sqrt(points)
    frequency = np.where(position < points // 2, position, position - points) / points
    propagator = np.conj(dft) @ (np.exp(-1j * np.pi * FRESNEL * frequency**2)[:, None] * dft)

    def split(matrix):
        high = matrix.astype(np.float32).astype(ml_dtypes.bfloat16)
        low = (matrix - high.astype(np.float64)).astype(np.float32).astype(ml_dtypes.bfloat16)
        return high, low

    lefts, rights = [], []
    for matrix in (propagator, np.conj(propagator), dft, np.conj(dft)):
        real, imag = matrix.real, matrix.imag
        high, low = split(np.block([[real, -imag], [imag, real]]))
        lefts.append(np.concatenate([high, high, low], axis=1))
        high, low = split(np.block([[real, imag], [-imag, real]]))
        rights.append(np.concatenate([high, high, low], axis=0))
    return np.stack(lefts), np.stack(rights)


def split(value):
    high = value.astype(jnp.bfloat16)
    return high, (value - high.astype(jnp.float32)).astype(jnp.bfloat16)


def grid(blocks):
    return jnp.concatenate([jnp.concatenate(row, axis=1) for row in blocks], axis=0)


def left_product(weight, pair):
    n = pair[0].shape[0]
    (r0, r0l), (r1, r1l), (i0, i0l), (i1, i1l) = map(split, pair)
    x = grid([[r0, r1], [i0, i1], [r0l, r1l], [i0l, i1l], [r0, r1], [i0, i1]])
    y = jnp.dot(weight, x, preferred_element_type=jnp.float32)
    return y[:n, :n], y[:n, n:], y[n:, :n], y[n:, n:]


def right_product(weight, pair):
    n = pair[0].shape[0]
    (r0, r0l), (r1, r1l), (i0, i0l), (i1, i1l) = map(split, pair)
    x = grid([[r0, i0, r0l, i0l, r0, i0], [r1, i1, r1l, i1l, r1, i1]])
    y = jnp.dot(x, weight, preferred_element_type=jnp.float32)
    return y[:n, :n], y[n:, :n], y[:n, n:], y[n:, n:]


def times(pair, obj):
    (r0, r1, i0, i1), (a, b) = pair, obj
    return r0 * a - i0 * b, r1 * a - i1 * b, r0 * b + i0 * a, r1 * b + i1 * a


def times_conj(pair, obj):
    return times(pair, (obj[0], -obj[1]))


def remote(source, target, send, recv, device):
    return pltpu.make_async_remote_copy(
        src_ref=source, dst_ref=target, send_sem=send, recv_sem=recv,
        device_id=device, device_id_type=pl.DeviceIdType.MESH,
    )


def signal(device):
    pl.semaphore_signal(
        pltpu.get_barrier_semaphore(), inc=1, device_id=device, device_id_type=pl.DeviceIdType.MESH
    )


def step(
    n_row, n_col, counts, offsets, obj, probe, amplitudes, lefts, rights, new_object, new_probe,
    ext0, ext1, ext2, ext3, acc, window, waves, side_in, edge_in, low_in, sums, first, middle, second, total,
    load, send, recv, col_send, col_recv, row_send, row_recv,
):
    a, b = lax.axis_index("row"), lax.axis_index("col")
    ext = (ext0, ext1, ext2, ext3)
    depth, rows, cols = obj.shape[1:]
    modes, n = probe.shape[1:3]
    pairs = modes // 2
    slots = amplitudes.shape[0]
    big = middle.shape[0]
    small = big // n_row
    has_up, has_down, has_left, has_right = a > 0, a < n_row - 1, b > 0, b < n_col - 1
    up, down, left, right = (a - 1, b), (a + 1, b), (a, b - 1), (a, b + 1)
    tile_r, tile_c, rim_r, rim_c = pl.ds(0, rows), pl.ds(0, cols), pl.ds(rows, n), pl.ds(cols, n)
    head = pl.ds(0, n)

    loads = [pltpu.make_async_copy(obj.at[:, s], ext[s].at[:, tile_r, tile_c], load.at[s]) for s in range(depth)]
    for copy in loads:
        copy.start()
    col_peers = [lax.rem(b + i, n_col) for i in range(1, n_col)]
    row_peers = [lax.rem(a + i, n_row) for i in range(1, n_row)]
    for peer in col_peers:
        signal((a, peer))
    for peer in row_peers:
        signal((peer, b))
    pl.semaphore_wait(pltpu.get_barrier_semaphore(), n_col - 1 + n_row - 1)

    def copies(kind, device, ends):
        return [remote(*ends(s), send.at[kind, s], recv.at[kind, s], device) for s in range(depth)]

    rows_out = copies(0, up, lambda s: (obj.at[:, s, head, :], ext[s].at[:, rim_r, tile_c]))
    side_out = copies(1, left, lambda s: (obj.at[:, s, :, head], ext[s].at[:, tile_r, rim_c]))
    edge_out = copies(2, left, lambda s: (ext[s].at[:, rim_r, head], ext[s].at[:, rim_r, rim_c]))
    side_back = copies(3, right, lambda s: (acc.at[:, s, tile_r, rim_c], side_in.at[:, s]))
    edge_back = copies(4, right, lambda s: (acc.at[:, s, rim_r, rim_c], edge_in.at[:, s]))
    rows_back = copies(5, down, lambda s: (acc.at[:, s, rim_r, tile_c], low_in.at[:, s]))

    for s in range(depth):

        @pl.when(has_up)
        def _():
            rows_out[s].start()

        @pl.when(has_left)
        def _():
            side_out[s].start()

    sums[...] = jnp.zeros_like(sums)

    acc[...] = jnp.zeros_like(acc)

    @pl.when(jnp.logical_not(has_down))
    def _():
        for ref in ext:
            ref[:, rim_r, tile_c] = jnp.zeros((2, n, cols), jnp.float32)

    @pl.when(jnp.logical_not(has_right))
    def _():
        for ref in ext:
            ref[:, tile_r, rim_c] = jnp.zeros((2, rows, n), jnp.float32)

    @pl.when(jnp.logical_not(has_down & has_right))
    def _():
        for ref in ext:
            ref[:, rim_r, rim_c] = jnp.zeros((2, n, n), jnp.float32)

    tall = n + ROWS
    lane = lax.broadcasted_iota(jnp.int32, (tall, n), 1)

    def place(k):
        return offsets[0, 0, k, 0] - a * rows, offsets[0, 0, k, 1] - b * cols

    def alive(k):
        return jnp.minimum(jnp.maximum(counts[0, 0] - k, 0), 1).astype(jnp.float32)

    def pick(amount, bit, clear, taken):
        return jnp.where(((jnp.zeros(clear.shape, jnp.int32) + amount) & bit) != 0, taken, clear)

    def turn(value, amount, axis, limit, sign):
        bit = 1
        while bit < limit:
            value = pick(amount, bit, value, pltpu.roll(value, sign * bit % value.shape[axis], axis))
            bit *= 2
        return value

    def keep(k, level, state):
        for p in range(pairs):
            for c in range(2):
                for j in range(2):
                    waves[k, level, c, 2 * p + j] = state[p][2 * c + j]

    def kept(k, level):
        source = probe if level < 0 else waves.at[k, level]
        return [tuple(source[c, 2 * p + j] for c in range(2) for j in range(2)) for p in range(pairs)]

    def product(which, state):
        state = [left_product(lefts[which], pair) for pair in state]
        return [right_product(rights[which], pair) for pair in state]

    def digits(low, size):
        return [low << i for i in range((size // low - 1).bit_length())]

    def cut(k, s):
        y, x = place(k)
        near = lane >= (jnp.zeros(lane.shape, jnp.int32) + x) & (n - 1)
        for c in range(2):
            value = ext[s][c]
            for bit in reversed(digits(n, cols)):
                value = pick(x, bit, value[:, :-bit], value[:, bit:])
            for bit in reversed(digits(ROWS, rows)):
                value = pick(y, bit, value[:-bit], value[bit:])
            value = turn(jnp.where(near, value[:, :n], value[:, n:]), x, 1, n, -1)
            window[k, c, s] = turn(value, y, 0, ROWS, -1)[:n]

    def scatter(k, c, s, grad):
        y, x = place(k)
        near = lane >= (jnp.zeros(lane.shape, jnp.int32) + x) & (n - 1)
        value = jnp.concatenate([grad, jnp.zeros((ROWS, n), jnp.float32)], axis=0)
        value = turn(turn(value, y, 0, ROWS, 1), x, 1, n, 1)
        value = jnp.concatenate([jnp.where(near, value, 0.0), jnp.where(near, 0.0, value)], axis=1)
        for bit in digits(ROWS, rows):
            gap = jnp.zeros((bit, value.shape[1]), jnp.float32)
            value = pick(y, bit, jnp.concatenate([value, gap], axis=0), jnp.concatenate([gap, value], axis=0))
        for bit in digits(n, cols):
            gap = jnp.zeros((value.shape[0], bit), jnp.float32)
            value = pick(x, bit, jnp.concatenate([value, gap], axis=1), jnp.concatenate([gap, value], axis=1))
        acc[c, s] += value

    def back(k, s, state):
        grads = [0.0, 0.0]
        for g, w in zip(state, kept(k, s - 1)):
            for j in range(2):
                grads[0] += g[j] * w[j] + g[2 + j] * w[2 + j]
                grads[1] += g[2 + j] * w[j] - g[j] * w[2 + j]
        for c in range(2):
            scatter(k, c, s, grads[c] * STEP_OBJECT)
        state = [times_conj(pair, (window[k, 0, s], window[k, 1, s])) for pair in state]
        if s > 0:
            keep(k, depth - 1, state)
        else:
            for p in range(pairs):
                for c in range(2):
                    for j in range(2):
                        sums[pl.ds((c * modes + 2 * p + j) * n, n)] += state[p][2 * c + j]

    def pass_down(s):
        @pl.when(has_down & has_left)
        def _():
            edge_back[s].wait_recv()
            acc[:, s, rim_r, head] += edge_in[:, s]

        @pl.when(has_down)
        def _():
            rows_back[s].start()

    for s in range(depth):
        loads[s].wait()

        @pl.when(has_down)
        def _():
            rows_out[s].wait_recv()

        @pl.when(has_down & has_left)
        def _():
            edge_out[s].start()

        @pl.when(has_right)
        def _():
            side_out[s].wait_recv()

        @pl.when(has_down & has_right)
        def _():
            edge_out[s].wait_recv()

        @pl.loop(0, slots)
        def _(k):
            cut(k, s)
            o = (window[k, 0, s], window[k, 1, s])
            if s == 0:
                sums[pl.ds(2 * modes * n, n)] += alive(k) * (o[0] ** 2 + o[1] ** 2)
            state = [times(pair, o) for pair in kept(k, s - 1)]
            if s < depth - 1:
                keep(k, s, product(0, state))
            else:
                state = product(2, state)
                intensity = sum(v * v for pair in state for v in pair)
                factor = alive(k) * (2.0 - 2.0 * amplitudes[k] / jnp.sqrt(intensity + 1.0))
                state = [tuple(v * factor for v in pair) for pair in state]
                back(k, s, product(3, state))

    for s in range(depth - 1, -1, -1):
        if s < depth - 1:

            @pl.loop(0, slots)
            def _(k):
                back(k, s, product(1, kept(k, depth - 1)))

            pass_down(s + 1)

        @pl.when(has_down & has_right)
        def _():
            edge_back[s].start()

        if s > 0:

            @pl.when(has_right)
            def _():
                side_back[s].start()

    def chunk(ref, index, size):
        return ref.at[pl.ds(pl.multiple_of(index * size, ROWS), size)]

    scatter_col = [
        remote(chunk(sums, peer, big), first.at[i], col_send.at[0, i], col_recv.at[0, i], (a, peer))
        for i, peer in enumerate(col_peers)
    ]
    for copy in scatter_col:
        copy.start()

    @pl.when(has_right)
    def _():
        side_back[0].start()

    pass_down(0)
    for s in range(depth):
        new_object[:, s] = ext[s][:, tile_r, tile_c] - acc[:, s, tile_r, tile_c]
    for copy in scatter_col:
        copy.wait()
    mine = chunk(sums, b, big)[...]
    for i in range(n_col - 1):
        mine += first[i]
    middle[...] = mine
    scatter_row = [
        remote(chunk(middle, peer, small), second.at[i], row_send.at[0, i], row_recv.at[0, i], (peer, b))
        for i, peer in enumerate(row_peers)
    ]
    for copy in scatter_row:
        copy.start()
    for copy in scatter_row:
        copy.wait()
    mine = chunk(middle, a, small)[...]
    for i in range(n_row - 1):
        mine += second[i]
    own = chunk(total, b * n_row + a, small)
    own[...] = mine
    gather_row = [
        remote(own, own, row_send.at[1, i], row_recv.at[1, i], (peer, b)) for i, peer in enumerate(row_peers)
    ]
    for copy in gather_row:
        copy.start()
    for copy in gather_row:
        copy.wait()
    group = chunk(total, b, big)
    gather_col = [
        remote(group, group, col_send.at[1, i], col_recv.at[1, i], (a, peer)) for i, peer in enumerate(col_peers)
    ]
    for copy in gather_col:
        copy.start()

    for s in range(depth - 1, -1, -1):

        @pl.when(has_left)
        def _():
            side_back[s].wait_recv()
            new_object[:, s, :, head] -= side_in[:, s]

        @pl.when(has_up)
        def _():
            rows_back[s].wait_recv()
            new_object[:, s, head, :] -= low_in[:, s]

    for copy in gather_col:
        copy.wait()
    scale = STEP_PROBE / (total[pl.ds(2 * modes * n, n)] + 1.0)
    for c in range(2):
        for m in range(modes):
            new_probe[c, m] = probe[c, m] - total[pl.ds((c * modes + m) * n, n)] * scale

    for s in range(depth):

        @pl.when(has_up)
        def _():
            rows_out[s].wait_send()

        @pl.when(has_left)
        def _():
            side_out[s].wait_send()

        @pl.when(has_down & has_left)
        def _():
            edge_out[s].wait_send()

        @pl.when(has_right)
        def _():
            side_back[s].wait_send()

        @pl.when(has_down & has_right)
        def _():
            edge_back[s].wait_send()

        @pl.when(has_down)
        def _():
            rows_back[s].wait_send()


def shards(n_row, n_col, object_field, probe, amplitudes, offsets, counts):
    _, depth, rows, cols = object_field.shape
    modes, n = probe.shape[1:3]
    slots = amplitudes.shape[2]
    f32 = jnp.float32
    vmem = pl.BlockSpec(memory_space=pltpu.VMEM)
    smem = pl.BlockSpec(memory_space=pltpu.SMEM)
    hbm = pl.BlockSpec(memory_space=pl.ANY)
    dma = pltpu.SemaphoreType.DMA
    lefts, rights = tables(n)
    devices = n_row * n_col
    small = -(-(2 * modes + 1) * n // (devices * ROWS)) * ROWS
    flops = slots * depth * 4 * 2 * (modes * n) * (6 * n) * (2 * n)
    return pl.pallas_call(
        partial(step, n_row, n_col),
        out_shape=(
            jax.ShapeDtypeStruct(object_field.shape, f32),
            jax.ShapeDtypeStruct(probe.shape, f32),
        ),
        in_specs=[smem, smem, hbm, vmem, vmem, vmem, vmem],
        out_specs=(vmem, vmem),
        scratch_shapes=[
            *[pltpu.VMEM((2, rows + n, cols + n), f32)] * 4,
            pltpu.VMEM((2, depth, rows + n, cols + n), f32),
            pltpu.VMEM((slots, 2, depth, n, n), f32),
            pltpu.VMEM((slots, depth, 2, modes, n, n), f32),
            pltpu.VMEM((2, depth, rows, n), f32),
            pltpu.VMEM((2, depth, n, n), f32),
            pltpu.VMEM((2, depth, n, cols), f32),
            pltpu.VMEM((devices * small, n), f32),
            pltpu.VMEM((n_col - 1, n_row * small, n), f32),
            pltpu.VMEM((n_row * small, n), f32),
            pltpu.VMEM((n_row - 1, small, n), f32),
            pltpu.VMEM((devices * small, n), f32),
            dma((depth,)),
            dma((6, depth)),
            dma((6, depth)),
            dma((2, n_col - 1)),
            dma((2, n_col - 1)),
            dma((2, n_row - 1)),
            dma((2, n_row - 1)),
        ],
        compiler_params=pltpu.CompilerParams(
            collective_id=0, has_side_effects=True, vmem_limit_bytes=56 * 2**20
        ),
        cost_estimate=pl.CostEstimate(flops=flops, bytes_accessed=8 * 2**20, transcendentals=0),
        name="step",
    )(counts, offsets, object_field, probe, amplitudes[0, 0], jnp.asarray(lefts), jnp.asarray(rights))


def solution(mesh):
    return jax.shard_map(
        partial(shards, mesh.shape["row"], mesh.shape["col"]),
        mesh=mesh,
        in_specs=(
            P(None, None, "row", "col"),
            P(),
            P("row", "col", None, None, None),
            P("row", "col", None, None),
            P("row", "col"),
        ),
        out_specs=(P(None, None, "row", "col"), P()),
        check_vma=False,
    )
```

```python
from functools import partial
import math

import jax
import jax.numpy as jnp
import ml_dtypes
import numpy as np
from jax import lax
from jax.experimental import pallas as pl
from jax.experimental.pallas import tpu as pltpu
from jax.sharding import PartitionSpec as P

FRESNEL = 4.0
STEP_OBJECT = 0.5
STEP_PROBE = 0.5
ROWS = 8


def tables(points):
    position = np.arange(points)
    angle = -2.0 * np.pi / points * (position[:, None] * position[None, :] % points)
    dft = np.exp(1j * angle) / math.sqrt(points)
    frequency = np.where(position < points // 2, position, position - points) / points
    propagator = np.conj(dft) @ (np.exp(-1j * np.pi * FRESNEL * frequency**2)[:, None] * dft)

    def split(matrix):
        high = matrix.astype(np.float32).astype(ml_dtypes.bfloat16)
        low = (matrix - high.astype(np.float64)).astype(np.float32).astype(ml_dtypes.bfloat16)
        return high, low

    lefts, rights = [], []
    for matrix in (propagator, np.conj(propagator), dft, np.conj(dft)):
        real, imag = matrix.real, matrix.imag
        high, low = split(np.block([[real, -imag], [imag, real]]))
        lefts.append(np.concatenate([high, high, low], axis=1))
        high, low = split(np.block([[real, imag], [-imag, real]]))
        rights.append(np.concatenate([high, high, low], axis=0))
    return np.stack(lefts), np.stack(rights)


def split(value):
    high = value.astype(jnp.bfloat16)
    return high, (value - high.astype(jnp.float32)).astype(jnp.bfloat16)


def grid(blocks):
    return jnp.concatenate([jnp.concatenate(row, axis=1) for row in blocks], axis=0)


def left_product(weight, pair):
    n = pair[0].shape[0]
    (r0, r0l), (r1, r1l), (i0, i0l), (i1, i1l) = map(split, pair)
    x = grid([[r0, r1], [i0, i1], [r0l, r1l], [i0l, i1l], [r0, r1], [i0, i1]])
    y = jnp.dot(weight, x, preferred_element_type=jnp.float32)
    return y[:n, :n], y[:n, n:], y[n:, :n], y[n:, n:]


def right_product(weight, pair):
    n = pair[0].shape[0]
    (r0, r0l), (r1, r1l), (i0, i0l), (i1, i1l) = map(split, pair)
    x = grid([[r0, i0, r0l, i0l, r0, i0], [r1, i1, r1l, i1l, r1, i1]])
    y = jnp.dot(x, weight, preferred_element_type=jnp.float32)
    return y[:n, :n], y[n:, :n], y[:n, n:], y[n:, n:]


def times(pair, obj):
    (r0, r1, i0, i1), (a, b) = pair, obj
    return r0 * a - i0 * b, r1 * a - i1 * b, r0 * b + i0 * a, r1 * b + i1 * a


def times_conj(pair, obj):
    return times(pair, (obj[0], -obj[1]))


def remote(source, target, send, recv, device):
    return pltpu.make_async_remote_copy(
        src_ref=source, dst_ref=target, send_sem=send, recv_sem=recv,
        device_id=device, device_id_type=pl.DeviceIdType.MESH,
    )


def signal(device):
    pl.semaphore_signal(
        pltpu.get_barrier_semaphore(), inc=1, device_id=device, device_id_type=pl.DeviceIdType.MESH
    )


def step(
    n_row, n_col, counts, offsets, obj, probe, amplitudes, lefts, rights, new_object, new_probe,
    ext0, ext1, ext2, ext3, acc, window, waves, flat, pad, side_in, edge_in, low_in, sums, first, middle, second, total,
    load, send, recv, col_send, col_recv, row_send, row_recv,
):
    a, b = lax.axis_index("row"), lax.axis_index("col")
    ext = (ext0, ext1, ext2, ext3)
    depth, rows, cols = obj.shape[1:]
    modes, n = probe.shape[1:3]
    pairs = modes // 2
    slots = amplitudes.shape[0]
    big = middle.shape[0]
    small = big // n_row
    has_up, has_down, has_left, has_right = a > 0, a < n_row - 1, b > 0, b < n_col - 1
    up, down, left, right = (a - 1, b), (a + 1, b), (a, b - 1), (a, b + 1)
    tile_r, tile_c, rim_r, rim_c = pl.ds(0, rows), pl.ds(0, cols), pl.ds(rows, n), pl.ds(cols, n)
    head = pl.ds(0, n)

    loads = [pltpu.make_async_copy(obj.at[:, s], ext[s].at[:, tile_r, tile_c], load.at[s]) for s in range(depth)]
    for copy in loads:
        copy.start()
    col_peers = [lax.rem(b + i, n_col) for i in range(1, n_col)]
    row_peers = [lax.rem(a + i, n_row) for i in range(1, n_row)]
    for peer in col_peers:
        signal((a, peer))
    for peer in row_peers:
        signal((peer, b))
    pl.semaphore_wait(pltpu.get_barrier_semaphore(), n_col - 1 + n_row - 1)

    def copies(kind, device, ends):
        return [remote(*ends(s), send.at[kind, s], recv.at[kind, s], device) for s in range(depth)]

    rows_out = copies(0, up, lambda s: (obj.at[:, s, head, :], ext[s].at[:, rim_r, tile_c]))
    side_out = copies(1, left, lambda s: (obj.at[:, s, :, head], ext[s].at[:, tile_r, rim_c]))
    edge_out = copies(2, left, lambda s: (ext[s].at[:, rim_r, head], ext[s].at[:, rim_r, rim_c]))
    side_back = copies(3, right, lambda s: (acc.at[:, s, tile_r, rim_c], side_in.at[:, s]))
    edge_back = copies(4, right, lambda s: (acc.at[:, s, rim_r, rim_c], edge_in.at[:, s]))
    rows_back = copies(5, down, lambda s: (acc.at[:, s, rim_r, tile_c], low_in.at[:, s]))

    for s in range(depth):

        @pl.when(has_up)
        def _():
            rows_out[s].start()

        @pl.when(has_left)
        def _():
            side_out[s].start()

    sums[...] = jnp.zeros_like(sums)


    @pl.loop(0, slots)
    def _(k):
        pad[k] = jnp.zeros_like(pad[k])

    @pl.when(jnp.logical_not(has_down))
    def _():
        for ref in ext:
            ref[:, rim_r, tile_c] = jnp.zeros((2, n, cols), jnp.float32)

    @pl.when(jnp.logical_not(has_right))
    def _():
        for ref in ext:
            ref[:, tile_r, rim_c] = jnp.zeros((2, rows, n), jnp.float32)

    @pl.when(jnp.logical_not(has_down & has_right))
    def _():
        for ref in ext:
            ref[:, rim_r, rim_c] = jnp.zeros((2, n, n), jnp.float32)

    tall = n + ROWS
    lead = rows // ROWS - 1
    lane = lax.broadcasted_iota(jnp.int32, (tall, n), 1)

    def place(k):
        return lax.rem(offsets[0, 0, k, 0], rows), lax.rem(offsets[0, 0, k, 1], cols)

    def alive(k):
        return jnp.minimum(jnp.maximum(counts[0, 0] - k, 0), 1).astype(jnp.float32)

    def pick(amount, bit, clear, taken):
        return jnp.where(((jnp.zeros(clear.shape, jnp.int32) + amount) & bit) != 0, taken, clear)

    def turn(value, amount, axis, limit, sign):
        bit = 1
        while bit < limit:
            value = pick(amount, bit, value, pltpu.roll(value, sign * bit % value.shape[axis], axis))
            bit *= 2
        return value

    def keep(k, level, state):
        for p in range(pairs):
            for c in range(2):
                for j in range(2):
                    waves[k, level, c, 2 * p + j] = state[p][2 * c + j]

    def kept(k, level):
        source = probe if level < 0 else waves.at[k, level]
        return [tuple(source[c, 2 * p + j] for c in range(2) for j in range(2)) for p in range(pairs)]

    def product(which, state):
        state = [left_product(lefts[which], pair) for pair in state]
        return [right_product(rights[which], pair) for pair in state]

    def cut(k, s):
        y, x = place(k)
        near = lane >= (jnp.zeros(lane.shape, jnp.int32) + x) & (n - 1)
        tile, block = lax.div(y, ROWS), lax.div(x, n)
        for c in range(2):
            first_block = jnp.concatenate([flat[c, block, tile + i] for i in range(tall // ROWS)], axis=0)
            next_block = jnp.concatenate([flat[c, block + 1, tile + i] for i in range(tall // ROWS)], axis=0)
            value = turn(jnp.where(near, first_block, next_block), x, 1, n, -1)
            window[k, c, s] = turn(value, y, 0, ROWS, -1)[:n]

    def scatter(k, c, s, grad):
        y, x = place(k)
        corner = jnp.zeros(lane.shape, jnp.int32) + x
        near = lane >= corner & (n - 1)
        block = corner - (corner & (n - 1)) + jnp.where(near, 0, n)
        value = jnp.concatenate([grad, jnp.zeros((ROWS, n), jnp.float32)], axis=0)
        value = turn(turn(value, y, 0, ROWS, 1), x, 1, n, 1)
        value = jnp.concatenate([jnp.where(block == start, value, 0.0) for start in range(0, cols + n, n)], axis=1)
        for i in range(tall // ROWS):
            pad[k, c, lead + i] = value[i * ROWS : (i + 1) * ROWS]

    def flatten(s):
        for c in range(2):
            for j in range((cols + n) // n):
                flat[c, j] = ext[s][c, :, j * n : (j + 1) * n].reshape((rows + n) // ROWS, ROWS, n)

    def add_up(s):
        starts = [lead - lax.div(place(k)[0], ROWS) for k in range(slots)]

        @pl.loop(0, (rows + n) // (4 * ROWS))
        def _(i):
            for c in range(2):
                for t in range(4):
                    value = pad[0, c, starts[0] + i * 4 + t]
                    for k in range(1, slots):
                        value += pad[k, c, starts[k] + i * 4 + t]
                    acc[c, s, pl.ds(pl.multiple_of((i * 4 + t) * ROWS, ROWS), ROWS), :] = value

    def back(k, s, state):
        grads = [0.0, 0.0]
        for g, w in zip(state, kept(k, s - 1)):
            for j in range(2):
                grads[0] += g[j] * w[j] + g[2 + j] * w[2 + j]
                grads[1] += g[2 + j] * w[j] - g[j] * w[2 + j]
        for c in range(2):
            scatter(k, c, s, grads[c] * STEP_OBJECT)
        state = [times_conj(pair, (window[k, 0, s], window[k, 1, s])) for pair in state]
        if s > 0:
            keep(k, depth - 1, state)
        else:
            for p in range(pairs):
                for c in range(2):
                    for j in range(2):
                        sums[pl.ds((c * modes + 2 * p + j) * n, n)] += state[p][2 * c + j]

    def pass_down(s):
        @pl.when(has_down & has_left)
        def _():
            edge_back[s].wait_recv()
            acc[:, s, rim_r, head] += edge_in[:, s]

        @pl.when(has_down)
        def _():
            rows_back[s].start()

    for s in range(depth):
        loads[s].wait()

        @pl.when(has_down)
        def _():
            rows_out[s].wait_recv()

        @pl.when(has_down & has_left)
        def _():
            edge_out[s].start()

        @pl.when(has_right)
        def _():
            side_out[s].wait_recv()

        @pl.when(has_down & has_right)
        def _():
            edge_out[s].wait_recv()

        flatten(s)

        @pl.loop(0, slots)
        def _(k):
            cut(k, s)
            o = (window[k, 0, s], window[k, 1, s])
            if s == 0:
                sums[pl.ds(2 * modes * n, n)] += alive(k) * (o[0] ** 2 + o[1] ** 2)
            state = [times(pair, o) for pair in kept(k, s - 1)]
            if s < depth - 1:
                keep(k, s, product(0, state))
            else:
                state = product(2, state)
                intensity = sum(v * v for pair in state for v in pair)
                factor = alive(k) * (2.0 - 2.0 * amplitudes[k] / jnp.sqrt(intensity + 1.0))
                state = [tuple(v * factor for v in pair) for pair in state]
                back(k, s, product(3, state))

    for s in range(depth - 1, -1, -1):
        if s < depth - 1:

            @pl.loop(0, slots)
            def _(k):
                back(k, s, product(1, kept(k, depth - 1)))

            pass_down(s + 1)
        add_up(s)

        @pl.when(has_down & has_right)
        def _():
            edge_back[s].start()

        if s > 0:

            @pl.when(has_right)
            def _():
                side_back[s].start()

    def chunk(ref, index, size):
        return ref.at[pl.ds(pl.multiple_of(index * size, ROWS), size)]

    scatter_col = [
        remote(chunk(sums, peer, big), first.at[i], col_send.at[0, i], col_recv.at[0, i], (a, peer))
        for i, peer in enumerate(col_peers)
    ]
    for copy in scatter_col:
        copy.start()

    @pl.when(has_right)
    def _():
        side_back[0].start()

    pass_down(0)
    for s in range(depth):
        new_object[:, s] = ext[s][:, tile_r, tile_c] - acc[:, s, tile_r, tile_c]
    for copy in scatter_col:
        copy.wait()
    mine = chunk(sums, b, big)[...]
    for i in range(n_col - 1):
        mine += first[i]
    middle[...] = mine
    scatter_row = [
        remote(chunk(middle, peer, small), second.at[i], row_send.at[0, i], row_recv.at[0, i], (peer, b))
        for i, peer in enumerate(row_peers)
    ]
    for copy in scatter_row:
        copy.start()
    for copy in scatter_row:
        copy.wait()
    mine = chunk(middle, a, small)[...]
    for i in range(n_row - 1):
        mine += second[i]
    own = chunk(total, b * n_row + a, small)
    own[...] = mine
    gather_row = [
        remote(own, own, row_send.at[1, i], row_recv.at[1, i], (peer, b)) for i, peer in enumerate(row_peers)
    ]
    for copy in gather_row:
        copy.start()
    for copy in gather_row:
        copy.wait()
    group = chunk(total, b, big)
    gather_col = [
        remote(group, group, col_send.at[1, i], col_recv.at[1, i], (a, peer)) for i, peer in enumerate(col_peers)
    ]
    for copy in gather_col:
        copy.start()

    for s in range(depth - 1, -1, -1):

        @pl.when(has_left)
        def _():
            side_back[s].wait_recv()
            new_object[:, s, :, head] -= side_in[:, s]

        @pl.when(has_up)
        def _():
            rows_back[s].wait_recv()
            new_object[:, s, head, :] -= low_in[:, s]

    for copy in gather_col:
        copy.wait()
    scale = STEP_PROBE / (total[pl.ds(2 * modes * n, n)] + 1.0)
    for c in range(2):
        for m in range(modes):
            new_probe[c, m] = probe[c, m] - total[pl.ds((c * modes + m) * n, n)] * scale

    for s in range(depth):

        @pl.when(has_up)
        def _():
            rows_out[s].wait_send()

        @pl.when(has_left)
        def _():
            side_out[s].wait_send()

        @pl.when(has_down & has_left)
        def _():
            edge_out[s].wait_send()

        @pl.when(has_right)
        def _():
            side_back[s].wait_send()

        @pl.when(has_down & has_right)
        def _():
            edge_back[s].wait_send()

        @pl.when(has_down)
        def _():
            rows_back[s].wait_send()


def shards(n_row, n_col, object_field, probe, amplitudes, offsets, counts):
    _, depth, rows, cols = object_field.shape
    modes, n = probe.shape[1:3]
    slots = amplitudes.shape[2]
    f32 = jnp.float32
    vmem = pl.BlockSpec(memory_space=pltpu.VMEM)
    smem = pl.BlockSpec(memory_space=pltpu.SMEM)
    hbm = pl.BlockSpec(memory_space=pl.ANY)
    dma = pltpu.SemaphoreType.DMA
    lefts, rights = tables(n)
    devices = n_row * n_col
    small = -(-(2 * modes + 1) * n // (devices * ROWS)) * ROWS
    flops = slots * depth * 4 * 2 * (modes * n) * (6 * n) * (2 * n)
    return pl.pallas_call(
        partial(step, n_row, n_col),
        out_shape=(
            jax.ShapeDtypeStruct(object_field.shape, f32),
            jax.ShapeDtypeStruct(probe.shape, f32),
        ),
        in_specs=[smem, smem, hbm, vmem, vmem, vmem, vmem],
        out_specs=(vmem, vmem),
        scratch_shapes=[
            *[pltpu.VMEM((2, rows + n, cols + n), f32)] * 4,
            pltpu.VMEM((2, depth, rows + n, cols + n), f32),
            pltpu.VMEM((slots, 2, depth, n, n), f32),
            pltpu.VMEM((slots, depth, 2, modes, n, n), f32),
            pltpu.VMEM((2, (cols + n) // n, (rows + n) // ROWS, ROWS, n), f32),
            pltpu.VMEM((slots, 2, (2 * rows + n) // ROWS - 1, ROWS, cols + n), f32),
            pltpu.VMEM((2, depth, rows, n), f32),
            pltpu.VMEM((2, depth, n, n), f32),
            pltpu.VMEM((2, depth, n, cols), f32),
            pltpu.VMEM((devices * small, n), f32),
            pltpu.VMEM((n_col - 1, n_row * small, n), f32),
            pltpu.VMEM((n_row * small, n), f32),
            pltpu.VMEM((n_row - 1, small, n), f32),
            pltpu.VMEM((devices * small, n), f32),
            dma((depth,)),
            dma((6, depth)),
            dma((6, depth)),
            dma((2, n_col - 1)),
            dma((2, n_col - 1)),
            dma((2, n_row - 1)),
            dma((2, n_row - 1)),
        ],
        compiler_params=pltpu.CompilerParams(
            collective_id=0, has_side_effects=True, vmem_limit_bytes=56 * 2**20
        ),
        cost_estimate=pl.CostEstimate(flops=flops, bytes_accessed=8 * 2**20, transcendentals=0),
        name="step",
    )(counts, offsets, object_field, probe, amplitudes[0, 0], jnp.asarray(lefts), jnp.asarray(rights))


def solution(mesh):
    return jax.shard_map(
        partial(shards, mesh.shape["row"], mesh.shape["col"]),
        mesh=mesh,
        in_specs=(
            P(None, None, "row", "col"),
            P(),
            P("row", "col", None, None, None),
            P("row", "col", None, None),
            P("row", "col"),
        ),
        out_specs=(P(None, None, "row", "col"), P()),
        check_vma=False,
    )
```
